32 devices in a mesh: req: 16 (over z, y, x), tp: 2 (over core).
Axes of the slice: x: 2, y: 2, z: 4, core: 2. Of those that a mesh axis runs over, the one named last changes fastest.
Arguments:
- hidden_in: bfloat16 [2048, 2048], P('req')
- attn_gain: float32 [2048], replicated, may hold values from 0.1 to 1.9
- w_query: bfloat16 [2048, 2048], P(None, 'tp'), may hold values from -0.125 to 0.125
- w_keyval: bfloat16 [2048, 4, 256], P(None, 'tp'), may hold values from -0.125 to 0.125
- w_out: bfloat16 [2048, 2048], P('tp'), may hold values from -0.125 to 0.125
- moe_gain: float32 [2048], replicated, may hold values from 0.1 to 1.9
- w_gate_up: bfloat16 [16, 2, 2048, 1408], P('req', None, None, 'tp'), may hold values from -0.125 to 0.125
- w_down: bfloat16 [16, 1408, 2048], P('req', 'tp'), may hold values from -0.15625 to 0.15625
- seg_ids: int32 [16, 128], P('req'), may hold values from 0 to 3, never falling along the last dimension, each value on 1 to 64 neighbouring positions
- cached_len: int32 [16], P('req'), may hold values from 2048 to 4096, as said below
- page_table: int32 [16, 32], P('req'), may hold values from 0 to 255, as said below
- cache_pool: bfloat16 [256, 4, 128, 256], P('req', 'tp')
- expert_ids: int32 [2048, 6], P('req'), may hold values from 0 to 15, all different within a row; in each aligned block of 128 rows (0 to 127, 128 to 255, ...) at most 64 rows name the same one
- expert_weights: float32 [2048, 6], P('req'), may hold values from 0.05 to 0.5
Outputs:
- layer_out: bfloat16 [2048, 2048], P('req')
The draws below stay inside these ranges and needn't reach their ends.
Inputs may be any that keep to these rules, and one draw needn't show every extreme that they name: `seg_ids`: row r holds the prompt numbers of pack r, never falling along the row; each prompt has 1 to 64 tokens, one exactly that many. `cached_len`: some pack has exactly 4096 cached tokens. `page_table`: entry j of row r names the page holding tokens j * 128 to (j + 1) * 128 - 1 of pack r's cached prefix; page p lies on index p // 16 of req. At most 4 entries of one row lie on one owner, and in every row some owner holds exactly 4. Entries past the cached length name pages too. `expert_ids`: each row names 6 different experts. Among the rows of one pack no expert is named more than 64 times, a bound that some block reaches.
All inputs are finite; a program needn't handle non-finite values.
Results may differ from the reference program's by a relative error of at most 0.009.
Values may be sent and summed in bfloat16 or wider, within the bound.
A program may use at most 128 MiB of HBM per device.

```python
import math
import jax
import jax.numpy as jnp
import numpy as np
from jax import lax

D = 2048
HEADS = 16
KV_HEADS = 4
HD = 128
FF = 1408
TOPK = 6
EXPERTS = 16
TOK_DEV = 128
SEGS = 4
PREF = 32
PAGE = 128
PAGES_DEV = 16
TOKENS = 2048
CAP_E = 64
N_REQ = 16


def draw_hidden_in(key, part):
    base_key, row_key, col_key = jax.random.split(key, 3)
    row_scale = jnp.exp(jax.random.uniform(row_key, (TOKENS, 1), jnp.float32, math.log(0.3), math.log(3.0)))
    col_scale = jnp.exp(jax.random.uniform(col_key, (1, D), jnp.float32, math.log(0.4), math.log(2.5)))
    raw_vals = jax.random.normal(base_key, (TOKENS, D), jnp.float32)
    return jnp.clip(raw_vals * row_scale * col_scale, -16.0, 16.0).astype(jnp.bfloat16)


def draw_cached_len(key, part):
    value_key, pick_key = jax.random.split(key, 2)
    lengths = jax.random.randint(value_key, (N_REQ,), PREF * PAGE // 2, PREF * PAGE + 1)
    chosen = jax.random.randint(pick_key, (), 0, N_REQ)
    return jnp.where(jnp.arange(N_REQ) == chosen, PREF * PAGE, lengths).astype(jnp.int32)


def owner_order(row_key):
    return jax.random.permutation(row_key, N_REQ)


def entry_order(row_key):
    return jax.random.permutation(row_key, PREF)


def draw_page_table(key, part):
    cap_pages = (2 * PREF + N_REQ - 1) // N_REQ
    owner_key, order_key, slot_key = jax.random.split(key, 3)
    owner_perm = jax.vmap(owner_order)(jax.random.split(owner_key, N_REQ))
    entry_perm = jax.vmap(entry_order)(jax.random.split(order_key, N_REQ))
    owners = jnp.take_along_axis(owner_perm, entry_perm // cap_pages, axis=1)
    slot_ids = jax.random.randint(slot_key, (N_REQ, PREF), 0, PAGES_DEV)
    return (owners * PAGES_DEV + slot_ids).astype(jnp.int32)


def draw_cache_pool(key, part):
    shape = (N_REQ * PAGES_DEV, KV_HEADS, PAGE, 2 * HD)
    base_key, scale_key, offset_key = jax.random.split(key, 3)
    dim_scale = jnp.exp(jax.random.uniform(scale_key, (1, KV_HEADS, 1, HD), jnp.float32, math.log(0.75), math.log(6.0)))
    value_offset = jax.random.normal(offset_key, (N_REQ * PAGES_DEV, KV_HEADS, 1, HD), jnp.float32)
    raw_vals = jax.random.normal(base_key, shape, jnp.float32)
    keys_part = raw_vals[..., :HD] * dim_scale
    values_part = 0.8 * raw_vals[..., HD:] + value_offset
    return jnp.concatenate([keys_part, values_part], axis=-1).astype(jnp.bfloat16)


def shard_levels(own_key, extent, shards, least, top_value):
    loudness = 1.0
    for position, parts in shards:
        heights = jax.random.uniform(jax.random.fold_in(jax.random.fold_in(own_key, 6), position), (parts,), jnp.float32, least / len(shards), top_value / len(shards))
        loudness = loudness * jnp.repeat(jnp.exp(heights), extent[position] // parts).reshape((-1,) + (1,) * (len(extent) - 1 - position))
    return loudness


def length_profile(count, total, reach, skew):
    loads = [(1 << 20) // math.isqrt(rank ** skew) + 1 for rank in range(2, count + 1)]
    surplus, given = total - reach - (count - 1), [1] * (count - 1)
    while surplus > 0:
        free = [i for i in range(count - 1) if given[i] < reach]
        mass, left = sum([loads[i] for i in free]), surplus
        for i in free:
            extra = min(reach - given[i], max(1, left * loads[i] // mass), surplus)
            given[i] = given[i] + extra
            surplus = surplus - extra
    return np.array([reach] + given)


def ragged(stream_key, number_of, total, reach, skew):
    if number_of == 2:
        one = jax.random.randint(stream_key, (), max(1, total - reach), min(reach, total - 1) + 1)
        return jnp.stack([one, total - one])
    tallies = jnp.asarray(length_profile(number_of, total, reach, skew), jnp.int32)
    couples = (number_of - 1) // 2
    donor, taker = tallies[1:1 + 2 * couples:2], tallies[2:2 + 2 * couples:2]
    margin = jnp.minimum(donor - 1, reach - taker)
    passed = jax.random.randint(jax.random.fold_in(stream_key, 1), (couples,), 0, 1 << 20) % (margin + 1)
    tallies = tallies.at[1:1 + 2 * couples:2].set(donor - passed).at[2:2 + 2 * couples:2].set(taker + passed)
    return tallies[jax.random.permutation(jax.random.fold_in(stream_key, 2), number_of)]


def deal_out(stream_key, own, number, rows, amount, top, reach, slope):
    sequence = jax.random.permutation(stream_key, amount)
    heavy_load, usual = portions_of(amount, rows * top, reach, slope, True), portions_of(amount, rows * top, reach, slope, False)
    places = jnp.arange(amount)

    def named(tallies, rotation):
        used = int((tallies > 0).sum())
        fixed = max(1, used // 4)
        moved = fixed + (places - fixed + rotation * (used - fixed)) % max(1, amount - fixed)
        return jnp.zeros((amount,), jnp.int32).at[sequence[jnp.where(places < fixed, places, moved)]].set(jnp.asarray(tallies, jnp.int32))

    tallies = jnp.where(number % 4 == 0, named(heavy_load, number // 4), named(usual, number - number // 4 - 1))
    mixed = jax.random.permutation(jax.random.fold_in(own, 3), amount)
    giver, receiver = mixed[0:amount // 2 * 2:2], mixed[1:amount // 2 * 2:2]
    room = jnp.minimum(tallies[giver] - 1, reach - tallies[receiver]) // 2
    room = jnp.where((giver == sequence[0]) | (receiver == sequence[0]) | (tallies[receiver] == 0), 0, jnp.maximum(room, 0))
    moved = jax.random.randint(jax.random.fold_in(own, 4), (amount // 2,), 0, 1 << 20) % (room + 1)
    tallies = tallies.at[giver].add(-moved).at[receiver].add(moved)
    labels = jnp.searchsorted(jnp.cumsum(tallies), jnp.arange(rows * top), side="right").astype(jnp.int32)
    listing = labels.reshape(top, rows).T
    listing = listing[jax.random.permutation(jax.random.fold_in(own, 1), rows)]
    rotation = jax.random.randint(jax.random.fold_in(own, 2), (rows, 1), 0, top)
    return jnp.take_along_axis(listing, (jnp.arange(top)[None, :] + rotation) % top, axis=1)


def portions_of(amount, total, reach, skew, full):
    portions = [(1 << 20) // math.isqrt(standing ** skew) + 1 for standing in range(1, amount + 1)]
    largest = reach if full else min(reach, max(-(-total // amount), total * portions[0] // sum(portions)))
    least = 1 if total - largest >= amount - 1 else 0
    given, rest = [largest] + [least] * (amount - 1), total - largest - least * (amount - 1)
    while rest > 0:
        movable = [i for i in range(1, amount) if given[i] < largest] or [i for i in range(1, amount) if given[i] < reach]
        pool, remaining = sum([portions[i] for i in movable]), rest
        for i in movable:
            more = min(reach - given[i], max(1, remaining * portions[i] // pool), rest)
            given[i] = given[i] + more
            rest = rest - more
    return np.array(given)


def centred(stream_key, shape, deviation, limit, shards=(), held_as=jnp.bfloat16):
    level = shard_levels(stream_key, shape, shards, -0.22, 0.18) if shards else 1.0
    drawn = jax.random.normal(stream_key, shape, jnp.float32) * deviation * level
    return jnp.minimum(jnp.maximum(drawn, -limit), limit).astype(held_as)


def setup_inputs(seed: int = 0) -> dict:
    seeds = jax.random.split(jax.random.key(seed), 15)
    hidden_in = draw_hidden_in(jax.random.fold_in(seeds[14], 71), 0)
    attn_gain = jnp.clip(1.0 + 0.18 * jax.random.normal(seeds[1], (D,), jnp.float32), 0.1, 1.9)
    w_query = centred(seeds[2], (D, HEADS * HD), D ** -0.5, 0.125, ((1, 2),))
    w_keyval = centred(seeds[3], (D, KV_HEADS, 2 * HD), D ** -0.5, 0.125, ((1, 2),))
    w_out = centred(seeds[4], (HEADS * HD, D), (HEADS * HD) ** -0.5, 0.125, ((0, 2),))
    moe_gain = jnp.clip(1.0 + 0.18 * jax.random.normal(seeds[5], (D,), jnp.float32), 0.1, 1.9)
    w_gate_up = centred(seeds[6], (EXPERTS, 2, D, FF), D ** -0.5, 0.125, ((0, 16), (3, 2)))
    w_down = centred(seeds[7], (EXPERTS, FF, D), FF ** -0.5, 0.15625, ((0, 16), (1, 2)))
    seg_ids = jax.vmap(lambda own: jnp.searchsorted(jnp.cumsum(ragged(own, SEGS, TOK_DEV, TOK_DEV // 2, 2)), jnp.arange(TOK_DEV), side="right"))(jax.random.split(seeds[8], N_REQ)).reshape((N_REQ, TOK_DEV)).astype(jnp.int32)
    cached_len = draw_cached_len(jax.random.fold_in(seeds[14], 71), 0)
    page_table = draw_page_table(jax.random.fold_in(seeds[14], 71), 0)
    cache_pool = draw_cache_pool(jax.random.fold_in(seeds[14], 71), 0)
    expert_ids_keys = jax.random.split(jax.random.fold_in(seeds[12], 1), TOKENS // TOK_DEV)
    expert_ids_turns = jax.random.permutation(jax.random.fold_in(seeds[12], 3), TOKENS // TOK_DEV)
    expert_ids = jax.vmap(lambda own, number: deal_out(jax.random.fold_in(seeds[12], 2), own, number, TOK_DEV, EXPERTS, TOPK, CAP_E, 2))(expert_ids_keys, expert_ids_turns).reshape((TOKENS, TOPK))
    expert_weights = jnp.clip(0.05 + 0.45 * jax.random.uniform(seeds[13], (TOKENS, TOPK), jnp.float32) ** shard_levels(seeds[13], (TOKENS, TOPK), ((0, 16),), -0.2, 0.2), 0.05, 0.5)
    return {"hidden_in": hidden_in, "attn_gain": attn_gain, "w_query": w_query, "w_keyval": w_keyval, "w_out": w_out, "moe_gain": moe_gain, "w_gate_up": w_gate_up, "w_down": w_down, "seg_ids": seg_ids, "cached_len": cached_len, "page_table": page_table, "cache_pool": cache_pool, "expert_ids": expert_ids, "expert_weights": expert_weights}


eps = 1e-06
rope_base = 600000.0

def rms_scale(rows_in, gain):
    widened = rows_in.astype(jnp.float32)
    return widened * lax.rsqrt(lax.optimization_barrier(jnp.mean(widened * widened, axis=-1, keepdims=True)) + eps) * gain

def rotate(vectors, angles):
    half_dim = vectors.shape[-1] // 2
    first_half = vectors[..., :half_dim]
    second_half = vectors[..., half_dim:]
    cosine = jnp.cos(angles)[:, None, :]
    sine_vals = jnp.sin(angles)[:, None, :]
    return jnp.concatenate([first_half * cosine - second_half * sine_vals, second_half * cosine + first_half * sine_vals], axis=-1)

def positions(segment_row, cached):
    length = segment_row.shape[0]
    token_index = jnp.arange(length, dtype=jnp.int32)
    begins = jnp.concatenate([jnp.ones((1,), dtype=bool), segment_row[1:] != segment_row[:-1]])
    seg_start = lax.cummax(jnp.where(begins, token_index, 0), axis=0)
    carried = segment_row == segment_row[0]
    place = token_index - seg_start + jnp.where(carried, cached, 0)
    return (place.astype(jnp.int32), carried)

def make_angles(place, head_dim):
    inverse = rope_base ** (-(jnp.arange(head_dim // 2, dtype=jnp.float32) * 2.0 / head_dim))
    return place.astype(jnp.float32)[:, None] * inverse[None, :]

def admit(segment_row, carried, cached, prefix_len):
    length = segment_row.shape[0]
    token_index = jnp.arange(length, dtype=jnp.int32)
    prefix_ok = (jnp.arange(prefix_len, dtype=jnp.int32)[None, :] < cached) & carried[:, None]
    local_ok = (segment_row[:, None] == segment_row[None, :]) & (token_index[None, :] <= token_index[:, None])
    return jnp.concatenate([prefix_ok, local_ok], axis=1)

def attend(queries, all_keys, all_values, admitted):
    scale = 1.0 / math.sqrt(queries.shape[-1])
    scores = jnp.einsum('tkgd,knd->kgtn', queries.astype(jnp.float32), all_keys.astype(jnp.float32)) * scale
    scores = jnp.where(admitted[None, None], scores, -1e+30)
    highest = lax.optimization_barrier(jnp.max(scores, axis=-1, keepdims=True))
    expo = jnp.exp(scores - highest)
    totals = lax.optimization_barrier(jnp.sum(expo, axis=-1, keepdims=True))
    weights = (expo / totals).astype(jnp.bfloat16)
    context = jnp.einsum('kgtn,knd->tkgd', weights.astype(jnp.float32), all_values.astype(jnp.float32))
    return context.astype(jnp.bfloat16)

def reference(hidden_in, attn_gain, w_query, w_keyval, w_out, moe_gain, w_gate_up, w_down, seg_ids, cached_len, page_table, cache_pool, expert_ids, expert_weights):
    normed = rms_scale(hidden_in, attn_gain).astype(jnp.bfloat16)
    place, carried = jax.vmap(positions)(seg_ids, cached_len)
    angles = make_angles(place.reshape(-1), HD)
    queries = jnp.dot(normed, w_query, preferred_element_type=jnp.float32).reshape(TOKENS, HEADS, HD)
    queries = rotate(queries, angles).astype(jnp.bfloat16)
    keyval = jnp.dot(normed, w_keyval.reshape(D, KV_HEADS * 2 * HD), preferred_element_type=jnp.float32).reshape(TOKENS, KV_HEADS, 2 * HD)
    keys_new = rotate(keyval[..., :HD], angles).astype(jnp.bfloat16)
    values_new = keyval[..., HD:].astype(jnp.bfloat16)

    def one_pack(packed):
        pack_queries, pack_keys, pack_values, segment_row, pack_carried, cached, table_row = packed
        pages = cache_pool[table_row]
        prefix = jnp.transpose(pages, (1, 0, 2, 3)).reshape(KV_HEADS, PREF * PAGE, 2 * HD)
        all_keys = jnp.concatenate([prefix[..., :HD], jnp.transpose(pack_keys, (1, 0, 2))], axis=1)
        all_values = jnp.concatenate([prefix[..., HD:], jnp.transpose(pack_values, (1, 0, 2))], axis=1)
        admitted = admit(segment_row, pack_carried, cached, PREF * PAGE)
        grouped = pack_queries.reshape(TOK_DEV, KV_HEADS, HEADS // KV_HEADS, HD)
        return attend(grouped, all_keys, all_values, admitted).reshape(TOK_DEV, HEADS * HD)
    contexts = lax.map(one_pack, (queries.reshape(N_REQ, TOK_DEV, HEADS, HD), keys_new.reshape(N_REQ, TOK_DEV, KV_HEADS, HD), values_new.reshape(N_REQ, TOK_DEV, KV_HEADS, HD), seg_ids, carried, cached_len, page_table))
    context = contexts.reshape(TOKENS, HEADS * HD)
    attention = jnp.dot(context, w_out, preferred_element_type=jnp.float32)
    resid = (hidden_in.astype(jnp.float32) + attention).astype(jnp.bfloat16)
    normed_moe = rms_scale(resid, moe_gain).astype(jnp.bfloat16)
    flat_ids = expert_ids.reshape(N_REQ, TOK_DEV * TOPK)
    onehot = (flat_ids[..., None] == jnp.arange(EXPERTS, dtype=jnp.int32)[None, None, :]).astype(jnp.int32)
    slot_rank = lax.optimization_barrier(jnp.sum((jnp.cumsum(onehot, axis=1) - 1) * onehot, axis=-1)).astype(jnp.int32)
    pack_index = jnp.broadcast_to(jnp.arange(N_REQ, dtype=jnp.int32)[:, None], flat_ids.shape)
    token_of = (jnp.arange(TOK_DEV * TOPK, dtype=jnp.int32)[None, :] // TOPK + pack_index * TOK_DEV).astype(jnp.int32)
    row_table = jnp.zeros((EXPERTS, N_REQ, CAP_E), jnp.int32).at[flat_ids, pack_index, slot_rank].set(token_of)
    weight_table = jnp.zeros((EXPERTS, N_REQ, CAP_E), jnp.float32).at[flat_ids, pack_index, slot_rank].set(expert_weights.reshape(N_REQ, TOK_DEV * TOPK))

    def expert_step(running, inputs):
        gate_up, down_proj, row_ids, slot_weights = inputs
        flat_rows = row_ids.reshape(-1)
        chosen = normed_moe[flat_rows]
        gate_part = jnp.dot(chosen, gate_up[0], preferred_element_type=jnp.float32)
        up_part = jnp.dot(chosen, gate_up[1], preferred_element_type=jnp.float32)
        hidden_act = (jax.nn.silu(gate_part) * up_part).astype(jnp.bfloat16)
        produced = jnp.dot(hidden_act, down_proj, preferred_element_type=jnp.float32).astype(jnp.bfloat16)
        running = running.at[flat_rows].add(slot_weights.reshape(-1)[:, None] * produced.astype(jnp.float32))
        return (running, None)
    moe_out, _ = lax.scan(expert_step, jnp.zeros((TOKENS, D), jnp.float32), (w_gate_up, w_down, row_table, weight_table))
    return (resid.astype(jnp.float32) + moe_out).astype(jnp.bfloat16)
```

```python
import functools
import math

import jax
import jax.numpy as jnp
from jax import lax
from jax.experimental import pallas as pl
from jax.experimental.pallas import tpu as pltpu
from jax.sharding import PartitionSpec as P

eps = 1e-06
rope_base = 600000.0
bf16 = jnp.bfloat16
f32 = jnp.float32
far = -1e30


def push_kernel(axis, n, scatter, place, count, *refs):
    ins, outs = refs[:count], refs[count : 2 * count]
    send, recv, own = refs[2 * count :]
    me = lax.axis_index(axis)
    barrier = pltpu.get_barrier_semaphore()
    for d in range(1, n):
        pl.semaphore_signal(
            barrier,
            inc=1,
            device_id={axis: lax.rem(me + d, n)},
            device_id_type=pl.DeviceIdType.MESH,
        )
    pl.semaphore_wait(barrier, n - 1)

    def source(x, p):
        if scatter == "lead":
            return x.at[p]
        if scatter == "cols":
            width = x.shape[-1] // n
            return x.at[:, pl.ds(pl.multiple_of(p * width, 128), width)]
        return x

    def target(o):
        if place == "cols":
            width = o.shape[-1] // n
            return o.at[:, pl.ds(pl.multiple_of(me * width, 128), width)]
        return o.at[me]

    copies = []
    for d in range(1, n):
        p = lax.rem(me + d, n)
        for k in range(count):
            c = pltpu.make_async_remote_copy(
                src_ref=source(ins[k], p),
                dst_ref=target(outs[k]),
                send_sem=send.at[k, d],
                recv_sem=recv.at[k, d],
                device_id={axis: p},
                device_id_type=pl.DeviceIdType.MESH,
            )
            c.start()
            copies.append(c)
    mine = []
    for k in range(count):
        c = pltpu.make_async_copy(source(ins[k], me), target(outs[k]), own.at[k])
        c.start()
        mine.append(c)
    for c in mine:
        c.wait()
    for c in copies:
        c.wait()


def push(xs, axis, ident, scatter=None, place="lead"):
    n = lax.axis_size(axis)
    count = len(xs)
    shapes = []
    for x in xs:
        block = x.shape
        if scatter == "lead":
            block = block[1:]
        if scatter == "cols":
            block = block[:-1] + (block[-1] // n,)
        whole = block[:-1] + (block[-1] * n,) if place == "cols" else (n,) + block
        shapes.append(jax.ShapeDtypeStruct(whole, x.dtype))
    return pl.pallas_call(
        functools.partial(push_kernel, axis, n, scatter, place, count),
        out_shape=shapes,
        in_specs=[pl.BlockSpec(memory_space=pl.ANY)] * count,
        out_specs=[pl.BlockSpec(memory_space=pl.ANY)] * count,
        scratch_shapes=[
            pltpu.SemaphoreType.DMA((count, n)),
            pltpu.SemaphoreType.DMA((count, n)),
            pltpu.SemaphoreType.DMA((count,)),
        ],
        compiler_params=pltpu.CompilerParams(collective_id=ident, has_side_effects=True),
        name="push_%d" % ident,
    )(*xs)


def owner_kernel(cap, kv, scale, slot_ref, valid_ref, q_ref, pool_ref, o_ref, stat_ref):
    p = pl.program_id(0)
    page = pool_ref.shape[2]
    hd = q_ref.shape[-1]
    rows = q_ref.shape[2]
    index = lax.broadcasted_iota(jnp.int32, (page, rows), 0)
    stat_ref[...] = jnp.zeros_like(stat_ref)
    for g in range(kv):
        q = q_ref[0, g]
        tops, scores = [], []
        for c in range(cap):
            keys = pool_ref[slot_ref[p, c], g, :, :hd]
            s = lax.dot_general(keys, q, (((1,), (1,)), ((), ())), preferred_element_type=f32)
            s = jnp.where(index < valid_ref[p, c], s * scale, far)
            scores.append(s)
            tops.append(jnp.max(s, axis=0, keepdims=True))
        top = functools.reduce(jnp.maximum, tops)
        total = jnp.zeros((1, rows), f32)
        acc = jnp.zeros((hd, rows), f32)
        for c in range(cap):
            e = jnp.where(index < valid_ref[p, c], jnp.exp(scores[c] - top), 0.0)
            total += jnp.sum(e, axis=0, keepdims=True)
            values = pool_ref[slot_ref[p, c], g, :, hd:]
            acc += lax.dot_general(
                values, e.astype(bf16), (((0,), (0,)), ((), ())), preferred_element_type=f32
            )
        o_ref[0, g] = (acc / jnp.where(total > 0, total, 1.0)).astype(bf16)
        stat_ref[0, 2 * g : 2 * g + 1] = top
        stat_ref[0, 2 * g + 1 : 2 * g + 2] = total


def owner_attend(slots, valid, q_all, pool):
    n, kv, rows, hd = q_all.shape
    cap = slots.shape[1]
    lines = -(-2 * kv // 8) * 8
    return pl.pallas_call(
        functools.partial(owner_kernel, cap, kv, 1.0 / math.sqrt(hd)),
        out_shape=[
            jax.ShapeDtypeStruct((n, kv, hd, rows), bf16),
            jax.ShapeDtypeStruct((n, lines, rows), f32),
        ],
        grid_spec=pltpu.PrefetchScalarGridSpec(
            num_scalar_prefetch=2,
            grid=(n,),
            in_specs=[
                pl.BlockSpec((1, kv, rows, hd), lambda p, *_: (p, 0, 0, 0)),
                pl.BlockSpec(pool.shape, lambda p, *_: (0, 0, 0, 0)),
            ],
            out_specs=[
                pl.BlockSpec((1, kv, hd, rows), lambda p, *_: (p, 0, 0, 0)),
                pl.BlockSpec((1, lines, rows), lambda p, *_: (p, 0, 0)),
            ],
        ),
        compiler_params=pltpu.CompilerParams(vmem_limit_bytes=40 * 2**20),
        name="owner_attend",
    )(slots, valid, q_all, pool)


def merge_kernel(n, kv, group, scale, q_ref, k_ref, v_ref, ok_ref, o_ref, stat_ref, out_ref):
    hd = k_ref.shape[-1]
    rows = q_ref.shape[2]
    half = rows // group
    for h in range(2):
        ok = ok_ref[h] > 0
        for g in range(kv):
            s = lax.dot_general(
                k_ref[g], q_ref[h, g], (((1,), (1,)), ((), ())), preferred_element_type=f32
            )
            s = jnp.where(ok, s * scale, far)
            top = jnp.max(s, axis=0, keepdims=True)
            if h == 0:
                flag = ok_ref[2, 0:1] > 0
                sums = [jnp.where(flag, stat_ref[i, 2 * g + 1 : 2 * g + 2], 0.0) for i in range(n)]
                tops = [
                    jnp.where(sums[i] > 0, stat_ref[i, 2 * g : 2 * g + 1], far) for i in range(n)
                ]
                top = functools.reduce(jnp.maximum, tops, top)
            e = jnp.where(ok, jnp.exp(s - top), 0.0)
            total = jnp.sum(e, axis=0, keepdims=True)
            acc = lax.dot_general(
                v_ref[g], e.astype(bf16), (((0,), (0,)), ((), ())), preferred_element_type=f32
            )
            if h == 0:
                for i in range(n):
                    share = jnp.exp(tops[i] - top) * sums[i]
                    total += share
                    acc += share * o_ref[i, g].astype(f32)
            context = (acc / total).T.astype(bf16)
            for j in range(group):
                head = g * group + j
                out_ref[h * half : (h + 1) * half, head * hd : (head + 1) * hd] = context[
                    j * half : (j + 1) * half
                ]


def merge(q_halves, keys, values, ok, shares, stats, group):
    n, kv, hd, rows = shares.shape
    tokens = 2 * rows // group
    return pl.pallas_call(
        functools.partial(merge_kernel, n, kv, group, 1.0 / math.sqrt(hd)),
        out_shape=jax.ShapeDtypeStruct((tokens, kv * group * hd), bf16),
        in_specs=[pl.BlockSpec(memory_space=pltpu.VMEM)] * 6,
        out_specs=pl.BlockSpec(memory_space=pltpu.VMEM),
        compiler_params=pltpu.CompilerParams(vmem_limit_bytes=40 * 2**20),
        name="merge",
    )(q_halves, keys, values, ok, shares, stats)


def rms_scale(rows_in, gain):
    widened = rows_in.astype(f32)
    return widened * lax.rsqrt(jnp.mean(widened * widened, axis=-1, keepdims=True) + eps) * gain


def rotate(vectors, angles):
    half_dim = vectors.shape[-1] // 2
    a, b = vectors[..., :half_dim], vectors[..., half_dim:]
    cosine, sine = jnp.cos(angles)[:, None, :], jnp.sin(angles)[:, None, :]
    return jnp.concatenate([a * cosine - b * sine, b * cosine + a * sine], axis=-1)


def shards(
    hidden_in,
    attn_gain,
    w_query,
    w_keyval,
    w_out,
    moe_gain,
    w_gate_up,
    w_down,
    seg_ids,
    cached_len,
    page_table,
    cache_pool,
    expert_ids,
    expert_weights,
):
    tok_rows, width = hidden_in.shape
    hd = w_keyval.shape[2] // 2
    kv = w_keyval.shape[1]
    q_local = w_query.shape[1] // hd
    group = q_local // kv
    half = tok_rows // 2
    n_req, n_tp = lax.axis_size("req"), lax.axis_size("tp")
    tp_me, req_me = lax.axis_index("tp"), lax.axis_index("req")
    part = width // n_tp
    seg, cached = seg_ids[0], cached_len[0]
    token = jnp.arange(tok_rows, dtype=jnp.int32)
    start = jnp.sum((seg[None, :] < seg[:, None]).astype(jnp.int32), axis=1)
    carried = seg == seg[0]
    place = token - start + jnp.where(carried, cached, 0)
    inverse = rope_base ** (-(jnp.arange(hd // 2, dtype=f32) * 2.0 / hd))
    angles = place.astype(f32)[:, None] * inverse[None, :]

    normed = rms_scale(hidden_in, attn_gain).astype(bf16)
    queries = jnp.dot(normed, w_query, preferred_element_type=f32).reshape(tok_rows, q_local, hd)
    queries = rotate(queries, angles).astype(bf16).reshape(2, half, kv, group, hd)
    q_halves = jnp.transpose(queries, (0, 2, 3, 1, 4)).reshape(2, kv, group * half, hd)

    pref = page_table.shape[1]
    info = jnp.concatenate([page_table[0], cached_len, jnp.zeros((127 - pref,), jnp.int32)])
    info = jnp.broadcast_to(info[None], (8, 128))
    q_all, info_all = push([q_halves[0], info], "req", 1)
    keyval = jnp.dot(normed, w_keyval.reshape(width, kv * 2 * hd), preferred_element_type=f32)
    keyval = keyval.reshape(tok_rows, kv, 2 * hd)
    keys_new = jnp.transpose(rotate(keyval[..., :hd], angles).astype(bf16), (1, 0, 2))
    values_new = jnp.transpose(keyval[..., hd:].astype(bf16), (1, 0, 2))

    pages_dev, page = cache_pool.shape[0], cache_pool.shape[2]
    cap = (2 * pref + n_req - 1) // n_req
    table, lengths = info_all[:, 0, :pref], info_all[:, 0, pref]
    here = (table // pages_dev) == req_me
    entry = jnp.arange(pref, dtype=jnp.int32)
    earlier = (entry[None, :] < entry[:, None])[None]
    rank = jnp.sum((here[:, None, :] & earlier).astype(jnp.int32), axis=2)
    ranks = jnp.arange(cap, dtype=jnp.int32)[None, :, None]
    chosen = here[:, None, :] & (rank[:, None, :] == ranks)
    slots = jnp.sum(jnp.where(chosen, (table % pages_dev)[:, None, :], 0), axis=2)
    room = jnp.clip(lengths[:, None] - entry[None, :] * page, 0, page)
    valid = jnp.sum(jnp.where(chosen, room[:, None, :], 0), axis=2)
    shares, stats = owner_attend(slots, valid, q_all, cache_pool)
    shares, stats = push([shares, stats], "req", 2, scatter="lead")

    local_ok = (seg[:, None] == seg[None, :]) & (token[:, None] <= token[None, :])
    local_ok = local_ok.astype(f32)
    flags = jnp.tile(carried[:half].astype(f32), (group,))[None]
    ok = jnp.stack(
        [
            jnp.tile(local_ok[:, :half], (1, group)),
            jnp.tile(local_ok[:, half:], (1, group)),
            jnp.broadcast_to(flags, (tok_rows, group * half)),
        ]
    )
    context = merge(q_halves, keys_new, values_new, ok, shares, stats, group)
    (sums,) = push([jnp.dot(context, w_out, preferred_element_type=f32)], "tp", 3)
    resid = (hidden_in.astype(f32) + jnp.sum(sums, axis=0)).astype(bf16)
    moe_in = rms_scale(resid, moe_gain).astype(bf16)

    topk = expert_ids.shape[1]
    n_exp = n_req * w_gate_up.shape[0]
    cap_e = 4 * tok_rows * topk // (3 * n_exp)
    named = expert_ids[:, :, None] == jnp.arange(n_exp, dtype=jnp.int32)[None, None, :]
    member = jnp.any(named, axis=1)
    weight = jnp.sum(jnp.where(named, expert_weights[:, :, None], 0.0), axis=1)
    before = (token[None, :] < token[:, None]).astype(bf16)
    row = jnp.dot(before, member.astype(bf16), preferred_element_type=f32).astype(jnp.int32)
    at = jnp.where(member, row, -1)
    picks = at.T[:, None, :] == jnp.arange(cap_e, dtype=jnp.int32)[None, :, None]
    selector = picks.reshape(n_exp * cap_e, tok_rows).astype(bf16)
    share_in = lax.dynamic_slice_in_dim(moe_in, tp_me * part, part, axis=1)
    outgoing = jnp.dot(selector, share_in, preferred_element_type=f32).astype(bf16)
    (arrived,) = push([outgoing.reshape(n_exp, cap_e, part)], "req", 4, scatter="lead")
    (rows_all,) = push([arrived.reshape(n_exp * cap_e, part)], "tp", 5, place="cols")
    gate = jnp.dot(rows_all, w_gate_up[0, 0], preferred_element_type=f32)
    up = jnp.dot(rows_all, w_gate_up[0, 1], preferred_element_type=f32)
    act = (jax.nn.silu(gate) * up).astype(bf16)
    made = jnp.dot(act, w_down[0], preferred_element_type=f32).astype(bf16)
    (halves,) = push([made], "tp", 6, scatter="cols")
    summed = jnp.sum(halves.astype(f32), axis=0).astype(bf16).reshape(n_req, cap_e, part)
    (results,) = push([summed], "req", 7, scatter="lead")
    spread = jnp.where(picks, weight.T[:, None, :], 0.0).reshape(n_exp * cap_e, tok_rows)
    high = spread.astype(bf16)
    low = (spread - high.astype(f32)).astype(bf16)
    results = results.reshape(n_exp * cap_e, part)
    contract = (((0,), (0,)), ((), ()))
    moe_out = lax.dot_general(high, results, contract, preferred_element_type=f32)
    moe_out += lax.dot_general(low, results, contract, preferred_element_type=f32)
    resid_part = lax.dynamic_slice_in_dim(resid, tp_me * part, part, axis=1)
    final = (resid_part.astype(f32) + moe_out).astype(bf16)
    (layer_out,) = push([final], "tp", 8, place="cols")
    return layer_out


def solution(mesh):
    in_specs = (
        P("req", None),
        P(),
        P(None, "tp"),
        P(None, "tp", None),
        P("tp", None),
        P(),
        P("req", None, None, "tp"),
        P("req", "tp", None),
        P("req", None),
        P("req"),
        P("req", None),
        P("req", "tp", None, None),
        P("req", None),
        P("req", None),
    )
    out_specs = P("req", None)
    return jax.shard_map(shards, mesh=mesh, in_specs=in_specs, out_specs=out_specs, check_vma=False)
```

```python
import functools
import math

import jax
import jax.numpy as jnp
from jax import lax
from jax.experimental import pallas as pl
from jax.experimental.pallas import tpu as pltpu
from jax.sharding import PartitionSpec as P

eps = 1e-06
rope_base = 600000.0
bf16 = jnp.bfloat16
f32 = jnp.float32
far = -1e30


def push_kernel(axis, n, scatter, place, count, *refs):
    ins, outs = refs[:count], refs[count : 2 * count]
    send, recv, own = refs[2 * count :]
    me = lax.axis_index(axis)
    barrier = pltpu.get_barrier_semaphore()
    for d in range(1, n):
        pl.semaphore_signal(
            barrier,
            inc=1,
            device_id={axis: lax.rem(me + d, n)},
            device_id_type=pl.DeviceIdType.MESH,
        )
    pl.semaphore_wait(barrier, n - 1)

    def source(x, p):
        if scatter == "lead":
            return x.at[p]
        if scatter == "cols":
            width = x.shape[-1] // n
            return x.at[:, pl.ds(pl.multiple_of(p * width, 128), width)]
        return x

    def target(o):
        if place == "cols":
            width = o.shape[-1] // n
            return o.at[:, pl.ds(pl.multiple_of(me * width, 128), width)]
        return o.at[me]

    copies = []
    for d in range(1, n):
        p = lax.rem(me + d, n)
        for k in range(count):
            c = pltpu.make_async_remote_copy(
                src_ref=source(ins[k], p),
                dst_ref=target(outs[k]),
                send_sem=send.at[k, d],
                recv_sem=recv.at[k, d],
                device_id={axis: p},
                device_id_type=pl.DeviceIdType.MESH,
            )
            c.start()
            copies.append(c)
    mine = []
    for k in range(count):
        c = pltpu.make_async_copy(source(ins[k], me), target(outs[k]), own.at[k])
        c.start()
        mine.append(c)
    for c in mine:
        c.wait()
    for c in copies:
        c.wait()


def push(xs, axis, ident, scatter=None, place="lead"):
    n = lax.axis_size(axis)
    count = len(xs)
    shapes = []
    for x in xs:
        block = x.shape
        if scatter == "lead":
            block = block[1:]
        if scatter == "cols":
            block = block[:-1] + (block[-1] // n,)
        whole = block[:-1] + (block[-1] * n,) if place == "cols" else (n,) + block
        shapes.append(jax.ShapeDtypeStruct(whole, x.dtype))
    return pl.pallas_call(
        functools.partial(push_kernel, axis, n, scatter, place, count),
        out_shape=shapes,
        in_specs=[pl.BlockSpec(memory_space=pltpu.VMEM)] * count,
        out_specs=[pl.BlockSpec(memory_space=pltpu.VMEM)] * count,
        scratch_shapes=[
            pltpu.SemaphoreType.DMA((count, n)),
            pltpu.SemaphoreType.DMA((count, n)),
            pltpu.SemaphoreType.DMA((count,)),
        ],
        compiler_params=pltpu.CompilerParams(
            collective_id=ident, has_side_effects=True, vmem_limit_bytes=40 * 2**20
        ),
        name="push_%d" % ident,
    )(*xs)


def owner_kernel(cap, kv, scale, slot_ref, valid_ref, q_ref, pool_ref, o_ref, stat_ref):
    p = pl.program_id(0)
    page = pool_ref.shape[2]
    hd = q_ref.shape[-1]
    rows = q_ref.shape[2]
    index = lax.broadcasted_iota(jnp.int32, (page, rows), 0)
    stat_ref[...] = jnp.zeros_like(stat_ref)
    for g in range(kv):
        q = q_ref[0, g]
        tops, scores = [], []
        for c in range(cap):
            keys = pool_ref[slot_ref[p, c], g, :, :hd]
            s = lax.dot_general(keys, q, (((1,), (1,)), ((), ())), preferred_element_type=f32)
            s = jnp.where(index < valid_ref[p, c], s * scale, far)
            scores.append(s)
            tops.append(jnp.max(s, axis=0, keepdims=True))
        top = functools.reduce(jnp.maximum, tops)
        total = jnp.zeros((1, rows), f32)
        acc = jnp.zeros((hd, rows), f32)
        for c in range(cap):
            e = jnp.where(index < valid_ref[p, c], jnp.exp(scores[c] - top), 0.0)
            total += jnp.sum(e, axis=0, keepdims=True)
            values = pool_ref[slot_ref[p, c], g, :, hd:]
            acc += lax.dot_general(
                values, e.astype(bf16), (((0,), (0,)), ((), ())), preferred_element_type=f32
            )
        o_ref[0, g] = (acc / jnp.where(total > 0, total, 1.0)).astype(bf16)
        stat_ref[0, 2 * g : 2 * g + 1] = top
        stat_ref[0, 2 * g + 1 : 2 * g + 2] = total


def owner_attend(slots, valid, q_all, pool):
    n, kv, rows, hd = q_all.shape
    cap = slots.shape[1]
    lines = -(-2 * kv // 8) * 8
    return pl.pallas_call(
        functools.partial(owner_kernel, cap, kv, 1.0 / math.sqrt(hd)),
        out_shape=[
            jax.ShapeDtypeStruct((n, kv, hd, rows), bf16),
            jax.ShapeDtypeStruct((n, lines, rows), f32),
        ],
        grid_spec=pltpu.PrefetchScalarGridSpec(
            num_scalar_prefetch=2,
            grid=(n,),
            in_specs=[
                pl.BlockSpec((1, kv, rows, hd), lambda p, *_: (p, 0, 0, 0)),
                pl.BlockSpec(pool.shape, lambda p, *_: (0, 0, 0, 0)),
            ],
            out_specs=[
                pl.BlockSpec((1, kv, hd, rows), lambda p, *_: (p, 0, 0, 0)),
                pl.BlockSpec((1, lines, rows), lambda p, *_: (p, 0, 0)),
            ],
        ),
        compiler_params=pltpu.CompilerParams(vmem_limit_bytes=40 * 2**20),
        name="owner_attend",
    )(slots, valid, q_all, pool)


def merge_kernel(n, kv, group, scale, q_ref, k_ref, v_ref, ok_ref, o_ref, stat_ref, out_ref):
    hd = k_ref.shape[-1]
    rows = q_ref.shape[2]
    half = rows // group
    for h in range(2):
        ok = ok_ref[h] > 0
        for g in range(kv):
            s = lax.dot_general(
                k_ref[g], q_ref[h, g], (((1,), (1,)), ((), ())), preferred_element_type=f32
            )
            s = jnp.where(ok, s * scale, far)
            top = jnp.max(s, axis=0, keepdims=True)
            if h == 0:
                flag = ok_ref[2, 0:1] > 0
                sums = [jnp.where(flag, stat_ref[i, 2 * g + 1 : 2 * g + 2], 0.0) for i in range(n)]
                tops = [
                    jnp.where(sums[i] > 0, stat_ref[i, 2 * g : 2 * g + 1], far) for i in range(n)
                ]
                top = functools.reduce(jnp.maximum, tops, top)
            e = jnp.where(ok, jnp.exp(s - top), 0.0)
            total = jnp.sum(e, axis=0, keepdims=True)
            acc = lax.dot_general(
                v_ref[g], e.astype(bf16), (((0,), (0,)), ((), ())), preferred_element_type=f32
            )
            if h == 0:
                for i in range(n):
                    share = jnp.exp(tops[i] - top) * sums[i]
                    total += share
                    acc += share * o_ref[i, g].astype(f32)
            context = (acc / total).T.astype(bf16)
            for j in range(group):
                head = g * group + j
                out_ref[h * half : (h + 1) * half, head * hd : (head + 1) * hd] = context[
                    j * half : (j + 1) * half
                ]


def merge(q_halves, keys, values, ok, shares, stats, group):
    n, kv, hd, rows = shares.shape
    tokens = 2 * rows // group
    return pl.pallas_call(
        functools.partial(merge_kernel, n, kv, group, 1.0 / math.sqrt(hd)),
        out_shape=jax.ShapeDtypeStruct((tokens, kv * group * hd), bf16),
        in_specs=[pl.BlockSpec(memory_space=pltpu.VMEM)] * 6,
        out_specs=pl.BlockSpec(memory_space=pltpu.VMEM),
        compiler_params=pltpu.CompilerParams(vmem_limit_bytes=40 * 2**20),
        name="merge",
    )(q_halves, keys, values, ok, shares, stats)


def rms_scale(rows_in, gain):
    widened = rows_in.astype(f32)
    return widened * lax.rsqrt(jnp.mean(widened * widened, axis=-1, keepdims=True) + eps) * gain


def rotate(vectors, angles):
    half_dim = vectors.shape[-1] // 2
    a, b = vectors[..., :half_dim], vectors[..., half_dim:]
    cosine, sine = jnp.cos(angles)[:, None, :], jnp.sin(angles)[:, None, :]
    return jnp.concatenate([a * cosine - b * sine, b * cosine + a * sine], axis=-1)


def shards(
    hidden_in,
    attn_gain,
    w_query,
    w_keyval,
    w_out,
    moe_gain,
    w_gate_up,
    w_down,
    seg_ids,
    cached_len,
    page_table,
    cache_pool,
    expert_ids,
    expert_weights,
):
    tok_rows, width = hidden_in.shape
    hd = w_keyval.shape[2] // 2
    kv = w_keyval.shape[1]
    q_local = w_query.shape[1] // hd
    group = q_local // kv
    half = tok_rows // 2
    n_req, n_tp = lax.axis_size("req"), lax.axis_size("tp")
    tp_me, req_me = lax.axis_index("tp"), lax.axis_index("req")
    part = width // n_tp
    seg, cached = seg_ids[0], cached_len[0]
    token = jnp.arange(tok_rows, dtype=jnp.int32)
    start = jnp.sum((seg[None, :] < seg[:, None]).astype(jnp.int32), axis=1)
    carried = seg == seg[0]
    place = token - start + jnp.where(carried, cached, 0)
    inverse = rope_base ** (-(jnp.arange(hd // 2, dtype=f32) * 2.0 / hd))
    angles = place.astype(f32)[:, None] * inverse[None, :]

    normed = rms_scale(hidden_in, attn_gain).astype(bf16)
    queries = jnp.dot(normed, w_query, preferred_element_type=f32).reshape(tok_rows, q_local, hd)
    queries = rotate(queries, angles).astype(bf16).reshape(2, half, kv, group, hd)
    q_halves = jnp.transpose(queries, (0, 2, 3, 1, 4)).reshape(2, kv, group * half, hd)

    pref = page_table.shape[1]
    info = jnp.concatenate([page_table[0], cached_len, jnp.zeros((127 - pref,), jnp.int32)])
    info = jnp.broadcast_to(info[None], (8, 128))
    q_all, info_all = push([q_halves[0], info], "req", 1)
    keyval = jnp.dot(normed, w_keyval.reshape(width, kv * 2 * hd), preferred_element_type=f32)
    keyval = keyval.reshape(tok_rows, kv, 2 * hd)
    keys_new = jnp.transpose(rotate(keyval[..., :hd], angles).astype(bf16), (1, 0, 2))
    values_new = jnp.transpose(keyval[..., hd:].astype(bf16), (1, 0, 2))

    pages_dev, page = cache_pool.shape[0], cache_pool.shape[2]
    cap = (2 * pref + n_req - 1) // n_req
    table, lengths = info_all[:, 0, :pref], info_all[:, 0, pref]
    here = (table // pages_dev) == req_me
    entry = jnp.arange(pref, dtype=jnp.int32)
    earlier = (entry[None, :] < entry[:, None])[None]
    rank = jnp.sum((here[:, None, :] & earlier).astype(jnp.int32), axis=2)
    ranks = jnp.arange(cap, dtype=jnp.int32)[None, :, None]
    chosen = here[:, None, :] & (rank[:, None, :] == ranks)
    slots = jnp.sum(jnp.where(chosen, (table % pages_dev)[:, None, :], 0), axis=2)
    room = jnp.clip(lengths[:, None] - entry[None, :] * page, 0, page)
    valid = jnp.sum(jnp.where(chosen, room[:, None, :], 0), axis=2)
    shares, stats = owner_attend(slots, valid, q_all, cache_pool)
    shares, stats = push([shares, stats], "req", 2, scatter="lead")

    local_ok = (seg[:, None] == seg[None, :]) & (token[:, None] <= token[None, :])
    local_ok = local_ok.astype(f32)
    flags = jnp.tile(carried[:half].astype(f32), (group,))[None]
    ok = jnp.stack(
        [
            jnp.tile(local_ok[:, :half], (1, group)),
            jnp.tile(local_ok[:, half:], (1, group)),
            jnp.broadcast_to(flags, (tok_rows, group * half)),
        ]
    )
    context = merge(q_halves, keys_new, values_new, ok, shares, stats, group)
    (sums,) = push([jnp.dot(context, w_out, preferred_element_type=f32)], "tp", 3)
    resid = (hidden_in.astype(f32) + jnp.sum(sums, axis=0)).astype(bf16)
    moe_in = rms_scale(resid, moe_gain).astype(bf16)

    topk = expert_ids.shape[1]
    n_exp = n_req * w_gate_up.shape[0]
    cap_e = 4 * tok_rows * topk // (3 * n_exp)
    named = expert_ids[:, :, None] == jnp.arange(n_exp, dtype=jnp.int32)[None, None, :]
    member = jnp.any(named, axis=1)
    weight = jnp.sum(jnp.where(named, expert_weights[:, :, None], 0.0), axis=1)
    before = (token[None, :] < token[:, None]).astype(bf16)
    row = jnp.dot(before, member.astype(bf16), preferred_element_type=f32).astype(jnp.int32)
    at = jnp.where(member, row, -1)
    picks = at.T[:, None, :] == jnp.arange(cap_e, dtype=jnp.int32)[None, :, None]
    selector = picks.reshape(n_exp * cap_e, tok_rows).astype(bf16)
    share_in = lax.dynamic_slice_in_dim(moe_in, tp_me * part, part, axis=1)
    outgoing = jnp.dot(selector, share_in, preferred_element_type=f32).astype(bf16)
    (arrived,) = push([outgoing.reshape(n_exp, cap_e, part)], "req", 4, scatter="lead")
    (rows_all,) = push([arrived.reshape(n_exp * cap_e, part)], "tp", 5, place="cols")
    gate = jnp.dot(rows_all, w_gate_up[0, 0], preferred_element_type=f32)
    up = jnp.dot(rows_all, w_gate_up[0, 1], preferred_element_type=f32)
    act = (jax.nn.silu(gate) * up).astype(bf16)
    made = jnp.dot(act, w_down[0], preferred_element_type=f32).astype(bf16)
    (halves,) = push([made], "tp", 6, scatter="cols")
    summed = jnp.sum(halves.astype(f32), axis=0).astype(bf16).reshape(n_req, cap_e, part)
    (results,) = push([summed], "req", 7, scatter="lead")
    spread = jnp.where(picks, weight.T[:, None, :], 0.0).reshape(n_exp * cap_e, tok_rows)
    high = spread.astype(bf16)
    low = (spread - high.astype(f32)).astype(bf16)
    results = results.reshape(n_exp * cap_e, part)
    contract = (((0,), (0,)), ((), ()))
    moe_out = lax.dot_general(high, results, contract, preferred_element_type=f32)
    moe_out += lax.dot_general(low, results, contract, preferred_element_type=f32)
    resid_part = lax.dynamic_slice_in_dim(resid, tp_me * part, part, axis=1)
    final = (resid_part.astype(f32) + moe_out).astype(bf16)
    (layer_out,) = push([final], "tp", 8, place="cols")
    return layer_out


def solution(mesh):
    in_specs = (
        P("req", None),
        P(),
        P(None, "tp"),
        P(None, "tp", None),
        P("tp", None),
        P(),
        P("req", None, None, "tp"),
        P("req", "tp", None),
        P("req", None),
        P("req"),
        P("req", None),
        P("req", "tp", None, None),
        P("req", None),
        P("req", None),
    )
    out_specs = P("req", None)
    return jax.shard_map(shards, mesh=mesh, in_specs=in_specs, out_specs=out_specs, check_vma=False)
```
